32 devices in a mesh: lat: 8 (over z, x), dep: 4 (over y, core).
Axes of the slice: x: 2, y: 2, z: 4, core: 2. Of those that a mesh axis runs over, the one named last changes fastest.
Arguments:
- kernel: bfloat16 [16384, 64, 128], P(('lat', 'dep')), may hold values from -0.1875 to 0.1875
- coefficient: float32 [16384, 256], P(('lat', 'dep')), may hold values from -3 to 3
- observed: float32 [2048, 64], P(('lat', 'dep')), may hold values from -6 to 6
- ray_brick: int32 [16384, 1], P(('lat', 'dep')), may hold values from 0 to 31; in each aligned block of 512 rows (0 to 511, 512 to 1023, ...) at most 24 rows name the same one
- tile_index: int32 [16384], P(('lat', 'dep')), may hold values from 0 to 511
- ray_count: int32 [32], P(('lat', 'dep')), may hold values from 32 to 64, as said below
- earth_model: float32 [32, 4, 512, 128], P(('lat', 'dep')), may hold values from -6 to 6
Outputs:
- residual: float32 [2048, 64], P(('lat', 'dep'))
- gradient: float32 [32, 4, 512, 128], P(('lat', 'dep'))
The draws below stay inside these ranges and needn't reach their ends.
Inputs may be any that keep to these rules, and one draw needn't show every extreme that they name: `ray_brick`: among the hits of one device no brick is named more than 24 times, a bound that some block reaches. `ray_count`: the largest count is exactly 64.
All inputs are finite; a program needn't handle non-finite values.
Results may differ from the reference program's by a relative error of at most 0.0037.
Values may be sent and summed in bfloat16 or wider, within the bound.
A program may use at most 64 MiB of HBM per device.

```python
import math
import jax
import jax.numpy as jnp
import numpy as np
from jax import lax

PARAMS = 4
BANDS = 64
CELLS = 128
TILES = 512
HITS_RAY = 8
RAYS_DEV = 64
BRICKS = 32
HITS_DEV = 512
CAP = 24
RAYS = 2048
HITS = 16384


def draw_ray_count(key, part):
    counts_drawn = jax.random.randint(key, (BRICKS,), RAYS_DEV // 2, RAYS_DEV + 1)
    fullest = jax.random.randint(jax.random.fold_in(key, 7), (), 0, BRICKS)
    return jnp.where(jnp.arange(BRICKS) == fullest, RAYS_DEV, counts_drawn).astype(jnp.int32)


def place_ends(drawn, key, smallest, largest):
    shape = drawn.shape
    spot = [jax.random.randint(jax.random.fold_in(key, axis), (), 0, shape[axis]) for axis in range(len(shape))]
    drawn = drawn.at[tuple(spot)].set(smallest)
    longest = shape.index(max(shape))
    spot[longest] = (spot[longest] + 1) % shape[longest]
    return drawn.at[tuple(spot)].set(largest)


def block_scale(key, extent, shards, smallest, largest):
    def one(position, parts):
        steps = jax.random.uniform(jax.random.fold_in(jax.random.fold_in(key, 6), position), (parts,), jnp.float32, smallest / len(shards), largest / len(shards))
        return jnp.repeat(jnp.exp(steps), extent[position] // parts).reshape((-1,) + (1,) * (len(extent) - position - 1))

    loudness = one(*shards[0])
    for cut in shards[1:]:
        loudness = loudness * one(*cut)
    return loudness


def shared_out(key, own, number, rows, amount, top, bound, skew):
    ranking = jax.random.permutation(key, amount)
    crowded, common = shares(amount, rows * top, bound, skew, True), shares(amount, rows * top, bound, skew, False)
    places = jnp.arange(amount)

    def named(lengths, turn):
        used = int((lengths > 0).sum())
        fixed = max(1, used // 4)
        shifted = fixed + (places - fixed + turn * (used - fixed)) % max(1, amount - fixed)
        return jnp.zeros((amount,), jnp.int32).at[ranking[jnp.where(places < fixed, places, shifted)]].set(jnp.asarray(lengths, jnp.int32))

    lengths = jnp.where(number % 4 == 0, named(crowded, number // 4), named(common, number - number // 4 - 1))
    mixed = jax.random.permutation(jax.random.fold_in(own, 3), amount)
    donor, sink = mixed[0:amount // 2 * 2:2], mixed[1:amount // 2 * 2:2]
    margin = jnp.minimum(lengths[donor] - 1, bound - lengths[sink]) // 2
    margin = jnp.where((donor == ranking[0]) | (sink == ranking[0]) | (lengths[sink] == 0), 0, jnp.maximum(margin, 0))
    shifted = jax.random.randint(jax.random.fold_in(own, 4), (amount // 2,), 0, 1 << 20) % (margin + 1)
    lengths = lengths.at[donor].add(-shifted).at[sink].add(shifted)
    members = jnp.searchsorted(jnp.cumsum(lengths), jnp.arange(rows * top), side="right").astype(jnp.int32)
    grid = members.reshape(top, rows).T
    grid = grid[jax.random.permutation(jax.random.fold_in(own, 1), rows)]
    turn = jax.random.randint(jax.random.fold_in(own, 2), (rows, 1), 0, top)
    return jnp.take_along_axis(grid, (jnp.arange(top)[None, :] + turn) % top, axis=1)


def shares(count, total, reach, lean, full):
    portions = [(1 << 20) // math.isqrt(grade ** lean) + 1 for grade in range(1, count + 1)]
    largest = reach if full else min(reach, max(-(-total // count), total * portions[0] // sum(portions)))
    least = 1 if total - largest >= count - 1 else 0
    given, surplus = [largest] + [least] * (count - 1), total - largest - least * (count - 1)
    while surplus > 0:
        free = [i for i in range(1, count) if given[i] < largest] or [i for i in range(1, count) if given[i] < reach]
        mass, left = sum([portions[i] for i in free]), surplus
        for i in free:
            addition = min(reach - given[i], max(1, left * portions[i] // mass), surplus)
            given[i] = given[i] + addition
            surplus = surplus - addition
    return np.array(given)


def noise(rng, shape, width, limit, cuts=(), kind=jnp.bfloat16):
    array = jax.random.normal(rng, shape, jnp.float32) * width
    if len(cuts) > 0:
        array = block_scale(rng, shape, cuts, -0.22, 0.18) * array
    return jnp.clip(array, min=-limit, max=limit).astype(kind)


def setup_inputs(seed: int = 0) -> dict:
    keys = jax.random.split(jax.random.key(seed), 8)
    kernel = noise(keys[0], (HITS, BANDS, CELLS), (CELLS * HITS_RAY) ** -0.5, 0.1875, ((0, 32),))
    coefficient = noise(keys[1], (HITS, PARAMS * BANDS), PARAMS ** -0.5, 3.0, ((0, 32),), jnp.float32)
    observed = noise(keys[2], (RAYS, BANDS), 1.0, 6.0, ((0, 32),), jnp.float32)
    ray_brick_keys = jax.random.split(jax.random.fold_in(keys[3], 1), HITS // HITS_DEV)
    ray_brick_turns = jax.random.permutation(jax.random.fold_in(keys[3], 3), HITS // HITS_DEV)
    ray_brick = jax.vmap(lambda own, number: shared_out(jax.random.fold_in(keys[3], 2), own, number, HITS_DEV, BRICKS, 1, CAP, 2))(ray_brick_keys, ray_brick_turns).reshape((HITS, 1))
    tile_index = place_ends(jax.random.randint(keys[4], (HITS,), 0, TILES), jax.random.fold_in(keys[4], 1), 0, TILES - 1).astype(jnp.int32)
    ray_count = draw_ray_count(jax.random.fold_in(keys[7], 71), 0)
    earth_model = noise(keys[6], (BRICKS, PARAMS, TILES, CELLS), 1.0, 6.0, ((0, 32),), jnp.float32)
    return dict(kernel=kernel, coefficient=coefficient, observed=observed, ray_brick=ray_brick, tile_index=tile_index, ray_count=ray_count, earth_model=earth_model)


def reference(kernel, coefficient, observed, ray_brick, tile_index, ray_count, earth_model):
    model_low = lax.optimization_barrier(earth_model.astype(jnp.bfloat16))
    kernel_split = kernel.reshape(BRICKS, HITS_DEV, BANDS, CELLS)
    coefficient_split = coefficient.reshape(BRICKS, HITS_DEV, PARAMS, BANDS)
    observed_split = observed.reshape(BRICKS, RAYS_DEV, BANDS)
    brick_split = ray_brick.reshape(BRICKS, HITS_DEV).astype(jnp.int32)
    tile_split = tile_index.reshape(BRICKS, HITS_DEV).astype(jnp.int32)

    def advance(gradient, inputs):
        kernel_block, coefficient_block, observed_block, brick_block, tile_block, live_count = inputs
        block = model_low[brick_block, :, tile_block, :].astype(jnp.float32)
        kernel_wide = kernel_block.astype(jnp.float32)
        sensitivity = jnp.einsum("hbc,hpc->hpb", kernel_wide, block)
        contribution = jnp.sum(coefficient_block * sensitivity, axis=1)
        predicted = jnp.sum(contribution.reshape(RAYS_DEV, HITS_RAY, BANDS), axis=1)
        live_rays = jnp.arange(RAYS_DEV) < live_count
        residual = jnp.where(live_rays[:, None], predicted - observed_block, jnp.zeros_like(predicted))
        residual_hit = jnp.repeat(residual, HITS_RAY, axis=0)
        weight = lax.optimization_barrier((coefficient_block * residual_hit[:, None, :]).astype(jnp.bfloat16))
        gradient_term = jnp.einsum("hpb,hbc->hpc", weight.astype(jnp.float32), kernel_wide)
        gradient = gradient.at[brick_block, :, tile_block, :].add(gradient_term)
        return gradient, residual

    start = jnp.zeros(earth_model.shape, jnp.float32)
    gradient, residual = lax.scan(advance, start, (kernel_split, coefficient_split, observed_split, brick_split, tile_split, ray_count))
    return residual.reshape(RAYS, BANDS), gradient
```

```python
import functools

import jax
import jax.numpy as jnp
from jax import lax
from jax.experimental import pallas as pl
from jax.experimental.pallas import tpu as pltpu
from jax.sharding import PartitionSpec as P

MESH = pl.DeviceIdType.MESH
F32 = jnp.float32
BF16 = jnp.bfloat16
GROUP = 8
UNROLL = 4


def tomography(
    lat_count,
    dep_count,
    slots,
    target_ref,
    tile_ref,
    count_ref,
    model_ref,
    coefficient_ref,
    observed_ref,
    kernel_hbm,
    residual_ref,
    gradient_ref,
    kernel_vmem,
    model_low,
    request_out,
    request_in,
    request_rows,
    pick,
    pick_t,
    place,
    place_t,
    model_out,
    model_in,
    model_rows,
    own,
    term,
    term_out,
    term_in,
    term_rows,
    kernel_sem,
    request_send,
    request_recv,
    model_send,
    model_recv,
    term_send,
    term_recv,
):
    devices = lat_count * dep_count
    params, tiles, cells = model_ref.shape
    hits = target_ref.shape[1]
    rays, bands = residual_ref.shape
    per_ray = hits // rays
    slot_total = devices * slots
    me = lax.axis_index("lat") * dep_count + lax.axis_index("dep")
    chunks = devices // GROUP
    group_rows = GROUP * slots

    def where_is(device):
        return (device // dep_count, device % dep_count)

    load = pltpu.make_async_copy(kernel_hbm, kernel_vmem, kernel_sem)
    load.start()

    barrier = pltpu.get_barrier_semaphore()

    @pl.loop(1, devices)
    def _(i):
        pl.semaphore_signal(
            barrier, inc=1, device_id=where_is((me + i) % devices), device_id_type=MESH
        )

    target = target_ref[...]
    tile = tile_ref[...]
    hit_lane = lax.broadcasted_iota(jnp.int32, (1, hits), 1)
    live = hit_lane < count_ref[0] * per_ray
    brick = lax.broadcasted_iota(jnp.int32, (devices, hits), 0)
    member = jnp.where((target == brick) & live, 1.0, 0.0).astype(F32)
    earlier = jnp.where(
        lax.broadcasted_iota(jnp.int32, (hits, hits), 0)
        < lax.broadcasted_iota(jnp.int32, (hits, hits), 1),
        1.0,
        0.0,
    ).astype(BF16)
    counted = jnp.dot(member.astype(BF16), earlier, preferred_element_type=F32)
    rank = jnp.sum(member * counted, axis=0, keepdims=True)
    ranked = jnp.where(
        lax.broadcasted_iota(jnp.int32, (128, hits), 0) == rank.astype(jnp.int32), 1.0, 0.0
    ).astype(BF16)
    high = (tile >> 5).astype(F32)
    low = (tile & 31).astype(F32) + 1.0
    dims = (((1,), (1,)), ((), ()))
    wanted = 32.0 * lax.dot_general(
        (member * high).astype(BF16), ranked, dims, preferred_element_type=F32
    ) + lax.dot_general((member * low).astype(BF16), ranked, dims, preferred_element_type=F32)
    for s in range(devices):
        request_out[s] = wanted[s : s + 1, :]

    pl.semaphore_wait(barrier, devices - 1)

    def request_copy(device, source):
        return pltpu.make_async_remote_copy(
            src_ref=request_out.at[device],
            dst_ref=request_in.at[source],
            send_sem=request_send.at[device],
            recv_sem=request_recv.at[source],
            device_id=where_is(device),
            device_id_type=MESH,
        )

    def model_copy(device, source):
        return pltpu.make_async_remote_copy(
            src_ref=model_out.at[device],
            dst_ref=model_in.at[source],
            send_sem=model_send.at[device],
            recv_sem=model_recv.at[source],
            device_id=where_is(device),
            device_id_type=MESH,
        )

    def term_copy(device, source):
        return pltpu.make_async_remote_copy(
            src_ref=term_out.at[device],
            dst_ref=term_in.at[source],
            send_sem=term_send.at[device],
            recv_sem=term_recv.at[source],
            device_id=where_is(device),
            device_id_type=MESH,
        )

    @pl.loop(0, devices)
    def _(i):
        device = (me + devices // 2 + i) % devices

        @pl.when(device != me)
        def _():
            request_copy(device, me).start()

    request_in[me] = request_out[me]

    slot = jnp.where(live, (target * slots).astype(F32) + rank, -1.0)
    for c in range(chunks):
        rows = lax.broadcasted_iota(jnp.int32, (group_rows, hits), 0) + c * group_rows
        place_t[c * group_rows : (c + 1) * group_rows, :] = jnp.where(
            rows.astype(F32) == slot, 1.0, 0.0
        ).astype(BF16)
    slot_column = jnp.transpose(jnp.broadcast_to(slot, (128, hits)))
    lane = lax.broadcasted_iota(jnp.int32, (hits, 128), 1).astype(F32)
    for m in range(slot_total // 128):
        place[:, m * 128 : (m + 1) * 128] = jnp.where(
            lane + float(m * 128) == slot_column, 1.0, 0.0
        ).astype(BF16)
    for p in range(params):
        model_low[:, p * cells : (p + 1) * cells] = model_ref[p].astype(BF16)
    request_rows[...] = jnp.zeros_like(request_rows)

    @pl.loop(1, devices)
    def _(i):
        request_copy((me + i) % devices, (me + i) % devices).wait_recv()

    for d in range(devices):
        request_rows[d : d + 1, :] = request_in[d]
    asked = jnp.transpose(request_rows[...])
    tile_lane = lax.broadcasted_iota(jnp.int32, (slots, tiles), 1).astype(F32) + 1.0
    for d in range(0, devices, 2):
        both = [
            jnp.where(asked[0:slots, e : e + 1] == tile_lane, 1.0, 0.0).astype(F32)
            for e in (d, d + 1)
        ]
        pick[d * slots : (d + 2) * slots, :] = jnp.concatenate(both, axis=0).astype(BF16)

    def send_group(step, matrix, values, out, back, copy):
        chunk = (me // GROUP + chunks // 2 + step) % chunks
        rows = pl.multiple_of(chunk * group_rows, group_rows)
        made = jnp.dot(
            matrix[pl.ds(rows, group_rows), :], values[...], preferred_element_type=F32
        )
        for k in range(GROUP):
            part = made[k * slots : (k + 1) * slots, :]
            block = jnp.concatenate(
                [part[:, p * cells : (p + 1) * cells] for p in range(params)], axis=0
            ).astype(BF16)
            out[chunk * GROUP + k] = block

        @pl.loop(0, GROUP)
        def _(k):
            device = chunk * GROUP + (me + k) % GROUP

            @pl.when(device != me)
            def _():
                copy(device, me).start()

            @pl.when(device == me)
            def _():
                back[me] = out[me]

    @pl.loop(0, chunks)
    def _(step):
        send_group(step, pick, model_low, model_out, model_in, model_copy)

    for m in range(slot_total // 128):
        pick_t[:, m * 128 : (m + 1) * 128] = jnp.transpose(
            pick[m * 128 : (m + 1) * 128, :].astype(F32)
        ).astype(BF16)

    def settle(blocks, rows_ref):
        @pl.loop(0, devices // 2)
        def _(i):
            both = []
            for e in range(2):
                block = blocks[2 * i + e].astype(F32)
                both.append(
                    jnp.concatenate(
                        [block[p * slots : (p + 1) * slots, :] for p in range(params)], axis=1
                    )
                )
            rows = pl.multiple_of(i * 2 * slots, 2 * slots)
            rows_ref[pl.ds(rows, 2 * slots), :] = jnp.concatenate(both, axis=0).astype(BF16)

    @pl.loop(1, devices)
    def _(i):
        model_copy((me + i) % devices, (me + i) % devices).wait_recv()

    settle(model_in, model_rows)

    @pl.loop(0, hits // 128)
    def _(i):
        rows = pl.multiple_of(i * 128, 128)
        own[pl.ds(rows, 128), :] = jnp.dot(
            place[pl.ds(rows, 128), :], model_rows[...], preferred_element_type=F32
        )

    load.wait()

    wide = per_ray * bands
    half = lax.broadcasted_iota(jnp.int32, (per_ray, 2 * bands), 1) < bands
    diagonal = (
        lax.broadcasted_iota(jnp.int32, (per_ray, wide), 1) // bands
        == lax.broadcasted_iota(jnp.int32, (per_ray, wide), 0)
    )

    def one_ray(ray):
        first = pl.multiple_of(ray * per_ray, per_ray)
        block = own[pl.ds(first, per_ray), :]
        block = jnp.concatenate(
            [block[:, p * cells : (p + 1) * cells] for p in range(params)], axis=0
        ).astype(BF16)
        tile_rows = pl.ds(pl.multiple_of(ray * wide, wide), wide)
        tile_block = kernel_vmem[tile_rows, :]
        coefficient = coefficient_ref[pl.ds(first, per_ray), :]
        spread = []
        for p in range(0, params, 2):
            pair = coefficient[:, p * bands : (p + 2) * bands]
            turned = pltpu.roll(pair, bands, 1)
            spread.append(jnp.where(half, pair, turned))
            spread.append(jnp.where(half, turned, pair))
        spread = [
            jnp.where(diagonal, jnp.concatenate([s] * (per_ray // 2), axis=1), 0.0) for s in spread
        ]
        spread = jnp.concatenate(spread, axis=0)
        sensitivity = lax.dot_general(block, tile_block, dims, preferred_element_type=F32)
        predicted = jnp.sum(spread * sensitivity, axis=0, keepdims=True)
        folded = predicted[:, 0 : 2 * bands]
        for k in range(1, per_ray // 2):
            folded = folded + predicted[:, 2 * bands * k : 2 * bands * (k + 1)]
        folded = folded + pltpu.roll(folded, bands, 1)
        observed = observed_ref[pl.ds(ray, 1), :]
        observed = jnp.concatenate([observed, observed], axis=1)
        residual = jnp.where(
            jnp.full(folded.shape, ray, jnp.int32) < count_ref[0], folded - observed, 0.0
        )
        residual_ref[pl.ds(ray, 1), :] = residual[:, 0:bands]
        weight = (spread * jnp.concatenate([residual] * (per_ray // 2), axis=1)).astype(BF16)
        back = jnp.dot(weight, tile_block, preferred_element_type=F32)
        return jnp.concatenate(
            [back[p * per_ray : (p + 1) * per_ray, :] for p in range(params)], axis=1
        )

    @pl.loop(0, rays // UNROLL)
    def _(i):
        made = jnp.concatenate([one_ray(i * UNROLL + u) for u in range(UNROLL)], axis=0)
        count = UNROLL * per_ray
        term[pl.ds(pl.multiple_of(i * count, count), count), :] = made.astype(BF16)

    @pl.loop(0, chunks)
    def _(step):
        send_group(step, place_t, term, term_out, term_in, term_copy)

    @pl.loop(1, devices)
    def _(i):
        device = (me + i) % devices
        request_copy(device, device).wait_send()
        model_copy(device, device).wait_send()

    @pl.loop(1, devices)
    def _(i):
        term_copy((me + i) % devices, (me + i) % devices).wait_recv()

    settle(term_in, term_rows)

    @pl.loop(0, tiles // 128)
    def _(i):
        rows = pl.multiple_of(i * 128, 128)
        summed = jnp.dot(
            pick_t[pl.ds(rows, 128), :], term_rows[...], preferred_element_type=F32
        )
        for p in range(params):
            gradient_ref[p, pl.ds(rows, 128), :] = summed[:, p * cells : (p + 1) * cells]

    @pl.loop(1, devices)
    def _(i):
        device = (me + i) % devices
        term_copy(device, device).wait_send()


def per_device(kernel, coefficient, observed, ray_brick, tile_index, ray_count, earth_model):
    hits, bands, cells = kernel.shape
    _, params, tiles, _ = earth_model.shape
    rays = observed.shape[0]
    lat_count = lax.axis_size("lat")
    dep_count = lax.axis_size("dep")
    devices = lat_count * dep_count
    cap = max(2, 3 * hits // (2 * devices))
    slots = -(-cap // 8) * 8
    total = devices * slots
    wide = params * cells
    vmem = pl.BlockSpec(memory_space=pltpu.VMEM)
    blocks = pltpu.VMEM((devices, params * slots, cells), BF16)
    sems = pltpu.SemaphoreType.DMA((devices,))
    residual, gradient = pl.pallas_call(
        functools.partial(tomography, lat_count, dep_count, slots),
        out_shape=(
            jax.ShapeDtypeStruct((rays, bands), F32),
            jax.ShapeDtypeStruct((params, tiles, cells), F32),
        ),
        in_specs=[
            vmem,
            vmem,
            pl.BlockSpec(memory_space=pltpu.SMEM),
            vmem,
            vmem,
            vmem,
            pl.BlockSpec(memory_space=pl.ANY),
        ],
        out_specs=(vmem, vmem),
        scratch_shapes=[
            pltpu.VMEM((hits * bands, cells), BF16),
            pltpu.VMEM((tiles, wide), BF16),
            pltpu.VMEM((devices, 1, 128), F32),
            pltpu.VMEM((devices, 1, 128), F32),
            pltpu.VMEM((-(-devices // 128) * 128, 128), F32),
            pltpu.VMEM((total, tiles), BF16),
            pltpu.VMEM((tiles, total), BF16),
            pltpu.VMEM((hits, total), BF16),
            pltpu.VMEM((total, hits), BF16),
            blocks,
            blocks,
            pltpu.VMEM((total, wide), BF16),
            pltpu.VMEM((hits, wide), F32),
            pltpu.VMEM((hits, wide), BF16),
            blocks,
            blocks,
            pltpu.VMEM((total, wide), BF16),
            pltpu.SemaphoreType.DMA,
            sems,
            sems,
            sems,
            sems,
            sems,
            sems,
        ],
        compiler_params=pltpu.CompilerParams(
            collective_id=0, has_side_effects=True, vmem_limit_bytes=56 * 1024 * 1024
        ),
        cost_estimate=pl.CostEstimate(
            flops=4 * hits * bands * cells * params, bytes_accessed=hits * bands * cells * 2, transcendentals=0
        ),
        name="tomography",
    )(
        ray_brick.reshape(1, hits),
        tile_index.reshape(1, hits),
        ray_count,
        earth_model[0],
        coefficient,
        observed,
        kernel.reshape(hits * bands, cells),
    )
    return residual, gradient[None]


def solution(mesh):
    return jax.shard_map(
        per_device,
        mesh=mesh,
        in_specs=(
            P(("lat", "dep"), None, None),
            P(("lat", "dep"), None),
            P(("lat", "dep"), None),
            P(("lat", "dep"), None),
            P(("lat", "dep")),
            P(("lat", "dep")),
            P(("lat", "dep"), None, None, None),
        ),
        out_specs=(P(("lat", "dep"), None), P(("lat", "dep"), None, None, None)),
        check_vma=False,
    )
```

```python
import functools

import jax
import jax.numpy as jnp
from jax import lax
from jax.experimental import pallas as pl
from jax.experimental.pallas import tpu as pltpu
from jax.sharding import PartitionSpec as P

MESH = pl.DeviceIdType.MESH
F32 = jnp.float32
BF16 = jnp.bfloat16
GROUP = 8
UNROLL = 8


def tomography(
    lat_count,
    dep_count,
    slots,
    target_ref,
    tile_ref,
    count_ref,
    model_hbm,
    coefficient_hbm,
    observed_hbm,
    kernel_hbm,
    residual_ref,
    gradient_ref,
    kernel_vmem,
    model_ref,
    coefficient_ref,
    observed_ref,
    model_low,
    request_out,
    request_in,
    request_rows,
    pick,
    pick_t,
    place,
    place_t,
    model_out,
    model_in,
    model_rows,
    own,
    term,
    term_out,
    term_in,
    load_sem,
    request_send,
    request_recv,
    model_send,
    model_recv,
    term_send,
    term_recv,
):
    devices = lat_count * dep_count
    params, tiles, cells = model_ref.shape
    hits = target_ref.shape[1]
    rays, bands = residual_ref.shape
    per_ray = hits // rays
    slot_total = devices * slots
    me = lax.axis_index("dep") * lat_count + lax.axis_index("lat")
    chunks = devices // GROUP
    group_rows = GROUP * slots

    def where_is(device):
        return (device % lat_count, device // lat_count)

    loads = [
        pltpu.make_async_copy(source, held, load_sem.at[i])
        for i, (source, held) in enumerate(
            [
                (model_hbm, model_ref),
                (coefficient_hbm, coefficient_ref),
                (observed_hbm, observed_ref),
                (kernel_hbm, kernel_vmem),
            ]
        )
    ]
    for load in loads:
        load.start()

    barrier = pltpu.get_barrier_semaphore()

    @pl.loop(1, devices)
    def _(i):
        pl.semaphore_signal(
            barrier, inc=1, device_id=where_is((me + i) % devices), device_id_type=MESH
        )

    target = target_ref[...]
    target = (target % dep_count) * lat_count + target // dep_count
    tile = tile_ref[...]
    hit_lane = lax.broadcasted_iota(jnp.int32, (1, hits), 1)
    live = hit_lane < count_ref[0] * per_ray
    brick = lax.broadcasted_iota(jnp.int32, (devices, hits), 0)
    member = jnp.where((target == brick) & live, 1.0, 0.0).astype(F32)
    earlier = jnp.where(
        lax.broadcasted_iota(jnp.int32, (hits, hits), 0)
        < lax.broadcasted_iota(jnp.int32, (hits, hits), 1),
        1.0,
        0.0,
    ).astype(BF16)
    counted = jnp.dot(member.astype(BF16), earlier, preferred_element_type=F32)
    rank = jnp.sum(member * counted, axis=0, keepdims=True)
    ranked = jnp.where(
        lax.broadcasted_iota(jnp.int32, (128, hits), 0) == rank.astype(jnp.int32), 1.0, 0.0
    ).astype(BF16)
    high = (tile >> 5).astype(F32)
    low = (tile & 31).astype(F32) + 1.0
    dims = (((1,), (1,)), ((), ()))
    wanted = 32.0 * lax.dot_general(
        (member * high).astype(BF16), ranked, dims, preferred_element_type=F32
    ) + lax.dot_general((member * low).astype(BF16), ranked, dims, preferred_element_type=F32)
    for s in range(devices):
        request_out[s] = wanted[s : s + 1, :]

    pl.semaphore_wait(barrier, devices - 1)

    def request_copy(device, source):
        return pltpu.make_async_remote_copy(
            src_ref=request_out.at[device],
            dst_ref=request_in.at[source],
            send_sem=request_send.at[device],
            recv_sem=request_recv.at[source],
            device_id=where_is(device),
            device_id_type=MESH,
        )

    def model_copy(device, source):
        return pltpu.make_async_remote_copy(
            src_ref=model_out.at[device],
            dst_ref=model_in.at[source],
            send_sem=model_send.at[device],
            recv_sem=model_recv.at[source],
            device_id=where_is(device),
            device_id_type=MESH,
        )

    def term_copy(device, source):
        return pltpu.make_async_remote_copy(
            src_ref=term_out.at[device],
            dst_ref=term_in.at[source],
            send_sem=term_send.at[device],
            recv_sem=term_recv.at[source],
            device_id=where_is(device),
            device_id_type=MESH,
        )

    @pl.loop(0, devices)
    def _(i):
        device = (me + devices // 2 + i) % devices

        @pl.when(device != me)
        def _():
            request_copy(device, me).start()

    request_in[me] = request_out[me]

    slot = jnp.where(live, (target * slots).astype(F32) + rank, -1.0)
    for c in range(chunks):
        rows = lax.broadcasted_iota(jnp.int32, (group_rows, hits), 0) + c * group_rows
        place_t[c * group_rows : (c + 1) * group_rows, :] = jnp.where(
            rows.astype(F32) == slot, 1.0, 0.0
        ).astype(BF16)
    loads[0].wait()
    for p in range(params):
        model_low[:, p * cells : (p + 1) * cells] = model_ref[p].astype(BF16)
    request_rows[...] = jnp.zeros_like(request_rows)

    @pl.loop(1, devices)
    def _(i):
        request_copy((me + i) % devices, (me + i) % devices).wait_recv()

    for d in range(devices):
        request_rows[d : d + 1, :] = request_in[d]
    asked = jnp.transpose(request_rows[...])
    tile_lane = lax.broadcasted_iota(jnp.int32, (slots, tiles), 1).astype(F32) + 1.0
    for d in range(0, devices, 2):
        both = [
            jnp.where(asked[0:slots, e : e + 1] == tile_lane, 1.0, 0.0).astype(F32)
            for e in (d, d + 1)
        ]
        pick[d * slots : (d + 2) * slots, :] = jnp.concatenate(both, axis=0).astype(BF16)

    def send_group(step, matrix, values, out, back, copy):
        chunk = (me // GROUP + chunks // 2 + step) % chunks
        rows = pl.multiple_of(chunk * group_rows, group_rows)
        made = jnp.dot(
            matrix[pl.ds(rows, group_rows), :], values[...], preferred_element_type=F32
        )
        for k in range(GROUP):
            part = made[k * slots : (k + 1) * slots, :]
            block = jnp.concatenate(
                [part[:, p * cells : (p + 1) * cells] for p in range(params)], axis=0
            ).astype(BF16)
            out[chunk * GROUP + k] = block

        @pl.loop(0, GROUP)
        def _(k):
            turn = 4 * ((k + 1) % 2) + 2 * ((k // 2) % 2) + k // 4
            device = chunk * GROUP + (me + turn) % GROUP

            @pl.when(device != me)
            def _():
                copy(device, me).start()

            @pl.when(device == me)
            def _():
                back[me] = out[me]

    @pl.loop(0, chunks)
    def _(step):
        send_group(step, pick, model_low, model_out, model_in, model_copy)

    slot_column = jnp.transpose(jnp.broadcast_to(slot, (256, hits)))[:, 0:group_rows]
    lane = lax.broadcasted_iota(jnp.int32, (hits, group_rows), 1).astype(F32)
    for c in range(chunks):
        place[c] = jnp.where(lane + float(c * group_rows) == slot_column, 1.0, 0.0).astype(BF16)
        pick_t[c] = jnp.transpose(
            pick[c * group_rows : (c + 1) * group_rows, :].astype(F32)
        ).astype(BF16)
    own[...] = jnp.zeros_like(own)

    def take_group(step, matrix, blocks, rows_ref, copy, add):
        chunk = (me // GROUP + chunks // 2 - step + chunks) % chunks

        @pl.loop(0, GROUP)
        def _(k):
            device = chunk * GROUP + k

            @pl.when(device != me)
            def _():
                copy(device, device).wait_recv()

        for k in range(0, GROUP, 2):
            both = []
            for e in range(2):
                block = blocks[chunk * GROUP + k + e].astype(F32)
                both.append(
                    jnp.concatenate(
                        [block[p * slots : (p + 1) * slots, :] for p in range(params)], axis=1
                    )
                )
            rows_ref[k * slots : (k + 2) * slots, :] = jnp.concatenate(both, axis=0).astype(BF16)

        @pl.loop(0, matrix.shape[1] // 128)
        def _(i):
            rows = pl.multiple_of(i * 128, 128)
            add(
                rows,
                jnp.dot(
                    matrix[chunk, pl.ds(rows, 128), :], rows_ref[...], preferred_element_type=F32
                ),
            )

    def add_own(rows, part):
        own[pl.ds(rows, 128), :] += part

    @pl.loop(0, chunks)
    def _(step):
        take_group(step, place, model_in, model_rows, model_copy, add_own)

    for load in loads[1:]:
        load.wait()

    wide = per_ray * bands
    half = lax.broadcasted_iota(jnp.int32, (per_ray, 2 * bands), 1) < bands
    diagonal = (
        lax.broadcasted_iota(jnp.int32, (per_ray, wide), 1) // bands
        == lax.broadcasted_iota(jnp.int32, (per_ray, wide), 0)
    )

    def one_ray(ray):
        first = pl.multiple_of(ray * per_ray, per_ray)
        block = own[pl.ds(first, per_ray), :]
        block = jnp.concatenate(
            [block[:, p * cells : (p + 1) * cells] for p in range(params)], axis=0
        ).astype(BF16)
        tile_rows = pl.ds(pl.multiple_of(ray * wide, wide), wide)
        tile_block = kernel_vmem[tile_rows, :]
        coefficient = coefficient_ref[pl.ds(first, per_ray), :]
        spread = []
        for p in range(0, params, 2):
            pair = coefficient[:, p * bands : (p + 2) * bands]
            turned = pltpu.roll(pair, bands, 1)
            spread.append(jnp.where(half, pair, turned))
            spread.append(jnp.where(half, turned, pair))
        spread = [
            jnp.where(diagonal, jnp.concatenate([s] * (per_ray // 2), axis=1), 0.0) for s in spread
        ]
        spread = jnp.concatenate(spread, axis=0)
        sensitivity = lax.dot_general(block, tile_block, dims, preferred_element_type=F32)
        predicted = jnp.sum(spread * sensitivity, axis=0, keepdims=True)
        folded = predicted[:, 0 : 2 * bands]
        for k in range(1, per_ray // 2):
            folded = folded + predicted[:, 2 * bands * k : 2 * bands * (k + 1)]
        folded = folded + pltpu.roll(folded, bands, 1)
        observed = observed_ref[pl.ds(ray, 1), :]
        observed = jnp.concatenate([observed, observed], axis=1)
        residual = jnp.where(
            jnp.full(folded.shape, ray, jnp.int32) < count_ref[0], folded - observed, 0.0
        )
        residual_ref[pl.ds(ray, 1), :] = residual[:, 0:bands]
        weight = (spread * jnp.concatenate([residual] * (per_ray // 2), axis=1)).astype(BF16)
        back = jnp.dot(weight, tile_block, preferred_element_type=F32)
        return jnp.concatenate(
            [back[p * per_ray : (p + 1) * per_ray, :] for p in range(params)], axis=1
        )

    @pl.loop(0, rays // UNROLL)
    def _(i):
        made = jnp.concatenate([one_ray(i * UNROLL + u) for u in range(UNROLL)], axis=0)
        count = UNROLL * per_ray
        term[pl.ds(pl.multiple_of(i * count, count), count), :] = made.astype(BF16)

    @pl.loop(0, chunks)
    def _(step):
        send_group(step, place_t, term, term_out, term_in, term_copy)

    @pl.loop(1, devices)
    def _(i):
        device = (me + i) % devices
        request_copy(device, device).wait_send()
        model_copy(device, device).wait_send()

    gradient_ref[...] = jnp.zeros_like(gradient_ref)

    def add_gradient(rows, part):
        for p in range(params):
            gradient_ref[p, pl.ds(rows, 128), :] += part[:, p * cells : (p + 1) * cells]

    @pl.loop(0, chunks)
    def _(step):
        take_group(step, pick_t, term_in, model_rows, term_copy, add_gradient)

    @pl.loop(1, devices)
    def _(i):
        device = (me + i) % devices
        term_copy(device, device).wait_send()


def per_device(kernel, coefficient, observed, ray_brick, tile_index, ray_count, earth_model):
    hits, bands, cells = kernel.shape
    _, params, tiles, _ = earth_model.shape
    rays = observed.shape[0]
    lat_count = lax.axis_size("lat")
    dep_count = lax.axis_size("dep")
    devices = lat_count * dep_count
    cap = max(2, 3 * hits // (2 * devices))
    slots = -(-cap // 8) * 8
    total = devices * slots
    wide = params * cells
    vmem = pl.BlockSpec(memory_space=pltpu.VMEM)
    blocks = pltpu.VMEM((devices, params * slots, cells), BF16)
    sems = pltpu.SemaphoreType.DMA((devices,))
    residual, gradient = pl.pallas_call(
        functools.partial(tomography, lat_count, dep_count, slots),
        out_shape=(
            jax.ShapeDtypeStruct((rays, bands), F32),
            jax.ShapeDtypeStruct((params, tiles, cells), F32),
        ),
        in_specs=[
            vmem,
            vmem,
            pl.BlockSpec(memory_space=pltpu.SMEM),
        ]
        + [pl.BlockSpec(memory_space=pl.ANY)] * 4,
        out_specs=(vmem, vmem),
        scratch_shapes=[
            pltpu.VMEM((hits * bands, cells), BF16),
            pltpu.VMEM((params, tiles, cells), F32),
            pltpu.VMEM((hits, params * bands), F32),
            pltpu.VMEM((rays, bands), F32),
            pltpu.VMEM((tiles, wide), BF16),
            pltpu.VMEM((devices, 1, 128), F32),
            pltpu.VMEM((devices, 1, 128), F32),
            pltpu.VMEM((-(-devices // 128) * 128, 128), F32),
            pltpu.VMEM((total, tiles), BF16),
            pltpu.VMEM((devices // GROUP, tiles, GROUP * slots), BF16),
            pltpu.VMEM((devices // GROUP, hits, GROUP * slots), BF16),
            pltpu.VMEM((total, hits), BF16),
            blocks,
            blocks,
            pltpu.VMEM((GROUP * slots, wide), BF16),
            pltpu.VMEM((hits, wide), F32),
            pltpu.VMEM((hits, wide), BF16),
            blocks,
            blocks,
            pltpu.SemaphoreType.DMA((4,)),
            sems,
            sems,
            sems,
            sems,
            sems,
            sems,
        ],
        compiler_params=pltpu.CompilerParams(
            collective_id=0, has_side_effects=True, vmem_limit_bytes=56 * 1024 * 1024
        ),
        cost_estimate=pl.CostEstimate(
            flops=4 * hits * bands * cells * params, bytes_accessed=hits * bands * cells * 2, transcendentals=0
        ),
        name="tomography",
    )(
        ray_brick.reshape(1, hits),
        tile_index.reshape(1, hits),
        ray_count,
        earth_model[0],
        coefficient,
        observed,
        kernel.reshape(hits * bands, cells),
    )
    return residual, gradient[None]


def solution(mesh):
    return jax.shard_map(
        per_device,
        mesh=mesh,
        in_specs=(
            P(("lat", "dep"), None, None),
            P(("lat", "dep"), None),
            P(("lat", "dep"), None),
            P(("lat", "dep"), None),
            P(("lat", "dep")),
            P(("lat", "dep")),
            P(("lat", "dep"), None, None, None),
        ),
        out_specs=(P(("lat", "dep"), None), P(("lat", "dep"), None, None, None)),
        check_vma=False,
    )
```
